256 devices in a mesh: grp: 8 (over z), tile: 32 (over y, x, core).
Axes of the slice: x: 4, y: 4, z: 8, core: 2. Of those that a mesh axis runs over, the one named last changes fastest.
Arguments:
- amplitudes: bfloat16 [2, 2048, 16384], P(None, ('grp', 'tile')), may hold values from -6 to 6
- integrals: bfloat16 [128, 128, 128, 128], P('tile', 'grp'), may hold values from -0.046875 to 0.046875
- tile_in: int32 [128, 128], P('tile'), may hold values from 0 to 127, each once within a row
- tile_list: int32 [2, 128, 128], P(None, 'tile'), may hold values from 0 to 127, as said below
- tile_count: int32 [2, 128], P(None, 'tile'), may hold values from 1 to 128, as said below
Outputs:
- ladder: bfloat16 [2, 2048, 16384], P(None, 'grp', 'tile')
The draws below stay inside these ranges and needn't reach their ends.
Inputs may be any that keep to these rules, and one draw needn't show every extreme that they name: Each row of tile_in names every input pair block once, so distinct tiles of one output block couple distinct input blocks. Entries of one row of tile_list are distinct; entries at j >= tile_count are ignored. `tile_count`: in each slab some block has exactly 128 live tiles.
All inputs are finite; a program needn't handle non-finite values.
Results may differ from the reference program's by a relative error of at most 0.001.
Values may be sent and summed in bfloat16 or wider, within the bound.
No kernel may reach another device: no remote copies, remote signals or barrier semaphores. Data moves between devices by JAX's collectives and lax.ppermute only.
A program may use at most 192 MiB of HBM per device.

```python
import jax
import jax.numpy as jnp
from jax import lax

TILE = 128
NBLK = 128
CAP = 128
POOLB = 128
OCC = 2048


def draw_tile_list(key, part):
    key = jax.random.fold_in(key, 11)
    keys = jax.random.split(key, 2 * NBLK)
    picked = jax.vmap(lambda single: jax.random.permutation(single, POOLB)[:CAP])(keys)
    return picked.reshape(2, NBLK, CAP).astype(jnp.int32)


def draw_tile_count(key, part):
    key = jax.random.fold_in(key, 23)
    first_key, second_key = jax.random.split(key)
    shifts = jax.random.randint(first_key, (2, NBLK), 0, 4)
    counts = jnp.maximum(jnp.right_shift(jnp.full((2, NBLK), CAP, jnp.int32), shifts), 1)
    fullest = jax.random.randint(second_key, (2, 1), 0, NBLK)
    counts = jnp.where(jnp.arange(NBLK)[None, :] == fullest, CAP, counts)
    return counts.astype(jnp.int32)


def shard_levels(stream_key, extent, cuts, smallest, top_value):
    gain, own = 1.0, jax.random.fold_in(stream_key, 6)
    for position, parts in cuts:
        draws = jnp.exp(jax.random.uniform(jax.random.fold_in(own, position), (parts,), jnp.float32, smallest / len(cuts), top_value / len(cuts)))
        gain = gain * jnp.repeat(draws, extent[position] // parts).reshape([-1 if axis == position else 1 for axis in range(len(extent))])
    return gain


def normal_values(rng, shape, spread, most, pieces=(), kind=jnp.bfloat16):
    array = spread * jax.random.normal(rng, shape, jnp.float32)
    if pieces:
        array = array * shard_levels(rng, shape, pieces, -0.22, 0.18)
    return jnp.clip(array, -most, most).astype(kind)


def setup_inputs(seed: int = 0) -> dict:
    seeds = jax.random.split(jax.random.key(seed), 6)
    return {
        "amplitudes": normal_values(seeds[0], (2, OCC, NBLK * TILE), 1.0, 6.0, ((1, 256),)),
        "integrals": normal_values(seeds[1], (NBLK, POOLB, TILE, TILE), (CAP * TILE) ** -0.5, 0.046875, ((0, 32), (1, 8))),
        "tile_in": jax.vmap(lambda own: jax.random.permutation(own, NBLK))(jax.random.split(seeds[2], NBLK)).reshape((NBLK, POOLB)).astype(jnp.int32),
        "tile_list": draw_tile_list(jax.random.fold_in(seeds[5], 71), 0),
        "tile_count": draw_tile_count(jax.random.fold_in(seeds[5], 71), 0),
    }


def reference(amplitudes, integrals, tile_in, tile_list, tile_count):
    columns = amplitudes.reshape(2, OCC, NBLK, TILE)

    def ladder_block(slab_block):
        slab_index, block_index = slab_block
        chosen = tile_list[slab_index, block_index]
        usable = (jnp.arange(CAP) < tile_count[slab_index, block_index]).astype(jnp.bfloat16)
        blocks = tile_in[block_index][chosen]
        packed_rows = jnp.take(columns[slab_index], blocks, axis=1).reshape(OCC, CAP * TILE)
        packed_tiles = (integrals[block_index][chosen] * usable[:, None, None]).reshape(CAP * TILE, TILE)
        product = jnp.dot(packed_rows, packed_tiles, preferred_element_type=jnp.float32)
        return (0.5 * product).astype(jnp.bfloat16)

    slab_all = jnp.repeat(jnp.arange(2, dtype=jnp.int32), NBLK)
    block_all = jnp.tile(jnp.arange(NBLK, dtype=jnp.int32), 2)
    result = lax.map(ladder_block, (slab_all, block_all))
    result = result.reshape(2, NBLK, OCC, TILE).transpose(0, 2, 1, 3)
    return result.reshape(2, OCC, NBLK * TILE)
```

```python
import functools

import jax
import jax.numpy as jnp
from jax import lax
from jax.experimental import pallas as pl
from jax.experimental.pallas import tpu as pltpu
from jax.sharding import PartitionSpec as P

WIDE = 8


def body(count, final, blocks, pool, ids, tile_in, live, *refs):
    amps = refs[:WIDE]
    tiles = refs[WIDE : WIDE + 2 * count]
    acc, out, total = refs[WIDE + 2 * count :]
    block, step = pl.program_id(0), pl.program_id(1)
    per_shard = 16 // WIDE

    @pl.when(step == 0)
    def _():
        total[...] = acc[...]

    start = ids[step // per_shard] * 16 + (step % per_shard) * WIDE

    def add(tile_ref):
        for slab in range(2):
            left = jnp.concatenate([a[slab] for a in amps], axis=1)
            picked = []
            for j in range(WIDE):
                on = live[(slab * blocks + block) * pool + start + j]
                tile = tile_ref[0, j]
                picked.append(jnp.where(on > 0, tile, jnp.zeros_like(tile)))
            right = jnp.concatenate(picked, axis=0)
            total[slab] += jnp.dot(left, right, preferred_element_type=jnp.float32)

    for shard in range(count):
        for half in range(2):
            here = (step // per_shard == shard) & (block // 2 == half)
            pl.when(here)(functools.partial(add, tiles[2 * shard + half]))

    @pl.when(step == pl.num_programs(1) - 1)
    def _():
        if final:
            out[...] = (0.5 * total[...]).astype(out.dtype)
        else:
            out[...] = total[...]


def accumulate(shards, ids, acc, amps, tile_in, live, final):
    count = len(shards)
    rows = amps.shape[1]
    blocks, pool = tile_in.shape
    per_shard = 16 // WIDE

    def amp_map(j, block, step, ids, tile_in, live):
        k = ids[step // per_shard] * 16 + (step % per_shard) * WIDE + j
        return 0, 0, tile_in[block * pool + k]

    def tile_map(shard, half, block, step, ids, tile_in, live):
        part = jnp.clip(step - shard * per_shard, 0, per_shard - 1)
        if half == 0:
            return jnp.minimum(block, 1), jnp.where(block < 2, part, per_shard - 1), 0, 0
        return jnp.maximum(block - 2, 0), jnp.where(block < 2, 0, part), 0, 0

    def own(block, step, ids, tile_in, live):
        return 0, 0, block

    specs = [pl.BlockSpec((2, rows, 128), functools.partial(amp_map, j)) for j in range(WIDE)]
    flat = []
    for shard, halves in enumerate(shards):
        for half in range(2):
            specs.append(pl.BlockSpec((1, WIDE, 128, 128), functools.partial(tile_map, shard, half)))
            flat.append(halves[half])
    specs.append(pl.BlockSpec((2, rows, 128), own))
    flops = 2 * 2 * rows * 128 * 128 * 16 * blocks * count
    moved = blocks * 16 * count * (2 * rows * 128 * 2 + 128 * 128 * 2)
    return pl.pallas_call(
        functools.partial(body, count, final, blocks, pool),
        out_shape=jax.ShapeDtypeStruct((2, rows, blocks * 128), jnp.bfloat16 if final else jnp.float32),
        grid_spec=pltpu.PrefetchScalarGridSpec(
            num_scalar_prefetch=3,
            grid=(blocks, count * per_shard),
            in_specs=specs,
            out_specs=pl.BlockSpec((2, rows, 128), own),
            scratch_shapes=[pltpu.VMEM((2, rows, 128), jnp.float32)],
        ),
        compiler_params=pltpu.CompilerParams(vmem_limit_bytes=32 * 1024 * 1024),
        cost_estimate=pl.CostEstimate(flops=flops, bytes_accessed=moved, transcendentals=0),
    )(ids, tile_in.reshape(-1), live.reshape(-1), *([amps] * WIDE), *flat, acc)


def on_device(groups, amplitudes, integrals, tile_in, tile_list, tile_count):
    pool = tile_in.shape[1]
    me = lax.axis_index("grp")
    plus = [(i, (i + 1) % groups) for i in range(groups)]
    minus = [(i, (i - 1) % groups) for i in range(groups)]

    amps = lax.all_gather(amplitudes, "tile", axis=1, tiled=True)

    slots = jnp.arange(tile_list.shape[-1], dtype=jnp.int32)
    listed = tile_list[..., None] == jnp.arange(pool, dtype=jnp.int32)
    within = (slots < tile_count[..., None])[..., None]
    live = jnp.any(listed & within, axis=2).astype(jnp.int32)

    low, high = integrals[:2], integrals[2:]
    held = {0: (low, high)}
    up, down = (low, high), (low, high)
    for step in range(1, 4):
        up = tuple(lax.ppermute(x, "grp", plus) for x in up)
        down = tuple(lax.ppermute(x, "grp", minus) for x in down)
        held[-step], held[step] = up, down
    held[4] = (lax.ppermute(up[0], "grp", plus), lax.ppermute(down[1], "grp", minus))

    acc = jnp.zeros((2, amps.shape[1], tile_in.shape[0] * 128), jnp.float32)
    for offsets in ((0, -1, 1), (-2, 2), (-3, 3), (4,)):
        ids = jnp.stack([(me + o) % groups for o in offsets]).astype(jnp.int32)
        acc = accumulate([held[o] for o in offsets], ids, acc, amps, tile_in, live, offsets == (4,))
    return acc


def solution(mesh):
    placed = (
        P(None, ("grp", "tile"), None),
        P("tile", "grp", None, None),
        P("tile", None),
        P(None, "tile", None),
        P(None, "tile"),
    )
    return jax.shard_map(
        functools.partial(on_device, mesh.shape["grp"]),
        mesh=mesh,
        in_specs=placed,
        out_specs=P(None, "grp", "tile"),
        check_vma=False,
    )
```

```python
import functools

import jax
import jax.numpy as jnp
from jax import lax
from jax.experimental import pallas as pl
from jax.experimental.pallas import tpu as pltpu
from jax.sharding import PartitionSpec as P

SIDE = 4
REL = (0, -1, 1, 2)
WIDE = 8


def swapped():
    return [(t, t ^ 1) for t in range(SIDE * SIDE * 2)]


def moved(phase, by):
    pairs = []
    for y in range(SIDE):
        for x in range(SIDE):
            for core in range(2):
                along_x = (phase + core) % 2 == 0
                to_y = y if along_x else (y + by) % SIDE
                to_x = (x + by) % SIDE if along_x else x
                pairs.append(((y * SIDE + x) * 2 + core, (to_y * SIDE + to_x) * 2 + core))
    return pairs


def turned(groups, tiles):
    half = groups // 2
    return [
        (g * tiles + t, ((g + half) % groups) * tiles + t)
        for g in range(groups)
        for t in range(tiles)
    ]


def body(pieces, low, tail, ordered, place, blocks_in, live, *refs):
    amps, tiles, out = refs[:pieces], refs[pieces:-1], refs[-1]
    block = low + pl.program_id(0)
    rows = 16 * 16
    first = lax.broadcasted_iota(jnp.int32, (16, 128), 0) < 8
    if tail is None:
        total = jnp.zeros((rows, 128), jnp.float32)
    else:
        tiles, total = tiles[:-1], tiles[-1][0]
    at = tail or 0
    for ref in tiles:
        for chunk in range(ref.shape[1] // WIDE):
            lefts = []
            for j in range(WIDE):
                entry = block * 64 + at + j
                column = pl.multiple_of(blocks_in[entry] * 128, 128)
                mask = jnp.where(first, live[2 * entry], live[2 * entry + 1]).astype(jnp.bfloat16)
                left = [(a[:, :, pl.ds(column, 128)] * mask[None]).reshape(-1, 128) for a in amps]
                lefts.append(jnp.concatenate(left, axis=0))
            left = jnp.concatenate(lefts, axis=1)
            right = ref[0, pl.ds(chunk * WIDE, WIDE)].reshape(WIDE * 128, 128)
            total += jnp.dot(left, right, preferred_element_type=jnp.float32)
            at += WIDE
    if ordered:
        for i in range(16):
            row = pl.multiple_of(place[i] * 16, 16)
            out[0, pl.ds(row, 16), :] = total[16 * i : 16 * (i + 1)]
    else:
        out[0] = total


def partial_ladder(group, amps, tiles, flips, tail, acc, ordered, place, blocks_in, live, low=0, high=8, light=1):
    rows = 256
    count = sum(x.shape[1] for x in tiles)

    def tile_map(flip, block, *_):
        return (low + block + 4 * flip) % 8, 0, 0, 0

    def out_map(block, *_):
        return block // 4, 0, block % 4

    specs = [pl.BlockSpec((2, *amps[0].shape[1:]), lambda *_: (group, 0, 0), pipeline_mode=pl.Buffered(1))] * len(amps)
    for x, flip in zip(tiles, flips, strict=True):
        specs.append(pl.BlockSpec((1, *x.shape[1:]), functools.partial(tile_map, flip)))
    if acc is not None:
        specs.append(pl.BlockSpec((1, rows, 128), out_map))
        tiles = [*tiles, acc]
    return pl.pallas_call(
        functools.partial(body, len(amps), low, tail, ordered),
        out_shape=jax.ShapeDtypeStruct(((high - low) // 4, rows, 512), jnp.float32),
        grid_spec=pltpu.PrefetchScalarGridSpec(
            num_scalar_prefetch=3,
            grid=(high - low,),
            in_specs=specs,
            out_specs=pl.BlockSpec((1, rows, 128), out_map),
        ),
        compiler_params=pltpu.CompilerParams(vmem_limit_bytes=24 * 1024 * 1024),
        cost_estimate=pl.CostEstimate(
            flops=2 * rows * count * 128 * 128 * (high - low) // light,
            bytes_accessed=(8 + count * (high - low) // 32) * 1024 * 1024 // light,
            transcendentals=0,
        ),
    )(place, blocks_in, live, *amps, *tiles)


def after(value, *done):
    return lax.optimization_barrier((value, done))[0]


def gather(shard, phase, steps):
    return [lax.ppermute(shard, "tile", moved(phase, step)) for step in steps]


def on_device(groups, tiles, amplitudes, integrals, tile_in, tile_list, tile_count):
    pool = tile_in.shape[1]
    me, tile = lax.axis_index("grp"), lax.axis_index("tile")
    y, x, core = tile // (2 * SIDE), (tile // 2) % SIDE, tile % 2
    plus = [(i, (i + 1) % groups) for i in range(groups)]
    minus = [(i, (i - 1) % groups) for i in range(groups)]
    both = ("grp", "tile")

    slots = jnp.arange(tile_list.shape[-1], dtype=jnp.int32)
    listed = tile_list[..., None] == jnp.arange(pool, dtype=jnp.int32)
    within = (slots < tile_count[..., None])[..., None]
    live = jnp.any(listed & within, axis=2).astype(jnp.int32)
    table = jnp.concatenate([tile_in[None], live], axis=0)
    other_table = lax.ppermute(table, "tile", swapped())
    table = jnp.concatenate([table, other_table], axis=1)
    table = jnp.roll(table, (2 - me) * 16, axis=2)
    low_near, high_near, low_half, high_half = (
        table[..., a:b] for a, b in ((16, 32), (48, 64), (8, 16), (64, 72))
    )
    zero = core == 0
    table = jnp.concatenate(
        [
            table[..., 32:48],
            jnp.where(zero, low_near, high_near),
            jnp.where(zero, high_near, low_near),
            jnp.where(zero, low_half, high_half),
            jnp.where(zero, high_half, low_half),
        ],
        axis=2,
    )
    blocks_in = table[0].reshape(-1)
    live = jnp.transpose(table[1:], (1, 2, 0)).reshape(-1).astype(jnp.float32)
    rel = jnp.array(REL, jnp.int32)
    along_1, along_2 = jnp.where(core == 0, x, y), jnp.where(core == 0, y, x)
    step_1, step_2 = jnp.where(core == 0, 1, SIDE), jnp.where(core == 0, SIDE, 1)
    place = ((along_2 + rel) % SIDE)[:, None] * step_2 + ((along_1 + rel) % SIDE)[None, :] * step_1
    place = place.reshape(-1).astype(jnp.int32)

    own = amplitudes.reshape(16, amplitudes.shape[-1])
    far = lax.ppermute(own, both, turned(groups, tiles))

    onward = [
        (g * tiles + t, ((g + (-1 if t % 2 else 1)) % groups) * tiles + t)
        for g in range(groups)
        for t in range(tiles)
    ]
    held = jnp.concatenate([integrals, lax.ppermute(integrals, "tile", swapped())], axis=0)
    own_near = gather(own, 0, (1, -1, 2))
    held, far, *own_near = lax.optimization_barrier((held, far, *own_near))
    near = lax.ppermute(held, both, onward)
    far_near = gather(far, 0, (1, -1, 2))
    fore = jnp.stack([own, own_near[0], far, far_near[0]])
    aft = jnp.stack([own_near[1], own_near[2], far_near[1], far_near[2]])
    fore_before = lax.ppermute(fore, "tile", moved(1, 1))
    aft_behind = lax.ppermute(aft, "tile", moved(1, -1))
    aft_before = lax.ppermute(aft, "tile", moved(1, 1))
    fore_behind = lax.ppermute(fore, "tile", moved(1, -1))
    fore_beyond = lax.ppermute(fore_before, "tile", moved(1, 1))
    aft_beyond = lax.ppermute(aft_behind, "tile", moved(1, -1))
    amps = [fore, aft, fore_before, aft_before, fore_behind, aft_behind, fore_beyond, aft_beyond]
    near = after(near, fore_before, aft_behind, fore_behind, aft_before)
    half = jnp.where(zero, near[:, 8:], near[:, :8])
    half = lax.ppermute(half, both, onward)
    near_other = lax.ppermute(near, "tile", swapped())

    facts = (place, blocks_in, live)
    first, flips, last_flips = [held, near, near_other], (0, 0, 1), (0, 1)
    back = partial_ladder(1, amps, first, flips, None, None, False, *facts)
    half_other = lax.ppermute(half, "tile", swapped())
    last = [half, half_other]
    back_1 = partial_ladder(1, amps, last, last_flips, 48, back[1:], True, *facts, low=4)
    back_1 = lax.ppermute(back_1[0].astype(jnp.float16), both, turned(groups, tiles))
    back_0 = partial_ladder(1, amps, last, last_flips, 48, back[:1], True, *facts, high=4)
    back_0 = lax.ppermute(back_0[0].astype(jnp.float16), both, turned(groups, tiles))
    every, flips = [*first, *last], (0, 0, 1, 0, 1)
    here_1 = partial_ladder(0, amps, every, flips, None, None, True, *facts, low=4)[0]
    here_0 = partial_ladder(0, amps, every, flips, None, None, True, *facts, high=4)[0]

    other = lax.ppermute((0.5 * (here_1 + back_1.astype(jnp.float32))).astype(jnp.bfloat16), "tile", swapped())
    same = (0.5 * (here_0 + back_0.astype(jnp.float32))).astype(jnp.bfloat16)
    even = jnp.where(zero, same, other).reshape(SIDE * SIDE, 2, 1, 8, 512)
    odd = jnp.where(zero, other, same).reshape(SIDE * SIDE, 2, 1, 8, 512)
    result = jnp.concatenate([even, odd], axis=2).transpose(1, 0, 2, 3, 4)
    return result.reshape(2, 256, 512)


def solution(mesh):
    placed = (
        P(None, ("grp", "tile"), None),
        P("tile", "grp", None, None),
        P("tile", None),
        P(None, "tile", None),
        P(None, "tile"),
    )
    return jax.shard_map(
        functools.partial(on_device, mesh.shape["grp"], mesh.shape["tile"]),
        mesh=mesh,
        in_specs=placed,
        out_specs=P(None, "grp", "tile"),
        check_vma=False,
    )
```

```python
import functools

import jax
import jax.numpy as jnp
from jax import lax
from jax.experimental import pallas as pl
from jax.experimental.pallas import tpu as pltpu
from jax.sharding import PartitionSpec as P

SIDE = 4
REL = (0, -1, 1, 2)
WIDE = 8


def swapped():
    return [(t, t ^ 1) for t in range(SIDE * SIDE * 2)]


def moved(phase, by):
    pairs = []
    for y in range(SIDE):
        for x in range(SIDE):
            for core in range(2):
                along_x = (phase + core) % 2 == 0
                to_y = y if along_x else (y + by) % SIDE
                to_x = (x + by) % SIDE if along_x else x
                pairs.append(((y * SIDE + x) * 2 + core, (to_y * SIDE + to_x) * 2 + core))
    return pairs


def turned(groups, tiles):
    half = groups // 2
    return [
        (g * tiles + t, ((g + half) % groups) * tiles + t)
        for g in range(groups)
        for t in range(tiles)
    ]


def body(pieces, low, tail, ordered, place, blocks_in, live, *refs):
    amps, tiles, out = refs[:pieces], refs[pieces:-1], refs[-1]
    block = low + pl.program_id(0)
    rows = 16 * 16
    first = lax.broadcasted_iota(jnp.int32, (16, 128), 0) < 8
    if tail is None:
        total = jnp.zeros((rows, 128), jnp.float32)
    else:
        tiles, total = tiles[:-1], tiles[-1][0]
    at = tail or 0
    for ref in tiles:
        for chunk in range(ref.shape[1] // WIDE):
            lefts = []
            for j in range(WIDE):
                entry = block * 64 + at + j
                column = pl.multiple_of(blocks_in[entry] * 128, 128)
                mask = jnp.where(first, live[2 * entry], live[2 * entry + 1]).astype(jnp.bfloat16)
                left = [(a[:, :, pl.ds(column, 128)] * mask[None]).reshape(-1, 128) for a in amps]
                lefts.append(jnp.concatenate(left, axis=0))
            left = jnp.concatenate(lefts, axis=1)
            right = ref[0, pl.ds(chunk * WIDE, WIDE)].reshape(WIDE * 128, 128)
            total += jnp.dot(left, right, preferred_element_type=jnp.float32)
            at += WIDE
    if ordered:
        for i in range(16):
            row = pl.multiple_of(place[i] * 16, 16)
            out[0, pl.ds(row, 16), :] = total[16 * i : 16 * (i + 1)]
    else:
        out[0] = total


def partial_ladder(amps, tiles, flips, tail, acc, ordered, place, blocks_in, live, low=0, high=8, light=1, pin=False):
    rows = 256
    count = sum(x.shape[1] for x in tiles)
    if pin:
        amps, tiles = ([pltpu.with_memory_space_constraint(x, pltpu.HBM) for x in xs] for xs in (amps, tiles))

    def tile_map(flip, block, *_):
        return (low + block + 4 * flip) % 8, 0, 0, 0

    def out_map(block, *_):
        return block // 4, 0, block % 4

    specs = [pl.BlockSpec(memory_space=pltpu.VMEM)] * len(amps)
    for x, flip in zip(tiles, flips, strict=True):
        specs.append(pl.BlockSpec((1, *x.shape[1:]), functools.partial(tile_map, flip)))
    if acc is not None:
        specs.append(pl.BlockSpec((1, rows, 128), out_map))
        tiles = [*tiles, acc]
    return pl.pallas_call(
        functools.partial(body, len(amps), low, tail, ordered),
        out_shape=jax.ShapeDtypeStruct(((high - low) // 4, rows, 512), jnp.float32),
        grid_spec=pltpu.PrefetchScalarGridSpec(
            num_scalar_prefetch=3,
            grid=(high - low,),
            in_specs=specs,
            out_specs=pl.BlockSpec((1, rows, 128), out_map),
        ),
        compiler_params=pltpu.CompilerParams(vmem_limit_bytes=24 * 1024 * 1024),
        cost_estimate=pl.CostEstimate(
            flops=2 * rows * count * 128 * 128 * (high - low) // light,
            bytes_accessed=(8 + count * (high - low) // 32) * 1024 * 1024 // light,
            transcendentals=0,
        ),
    )(place, blocks_in, live, *amps, *tiles)


def after(value, *done):
    return lax.optimization_barrier((value, done))[0]


def gather(shard, phase, steps):
    return [lax.ppermute(shard, "tile", moved(phase, step)) for step in steps]


def spread(own, before, behind, opposite):
    fore, aft = jnp.stack([own, before]), jnp.stack([behind, opposite])
    fore_before = lax.ppermute(fore, "tile", moved(1, 1))
    aft_behind = lax.ppermute(aft, "tile", moved(1, -1))
    aft_before = lax.ppermute(aft, "tile", moved(1, 1))
    fore_behind = lax.ppermute(fore, "tile", moved(1, -1))
    fore_beyond = lax.ppermute(fore_before, "tile", moved(1, 1))
    aft_beyond = lax.ppermute(aft_behind, "tile", moved(1, -1))
    return [fore, aft, fore_before, aft_before, fore_behind, aft_behind, fore_beyond, aft_beyond]


def on_device(groups, tiles, amplitudes, integrals, tile_in, tile_list, tile_count):
    pool = tile_in.shape[1]
    me, tile = lax.axis_index("grp"), lax.axis_index("tile")
    y, x, core = tile // (2 * SIDE), (tile // 2) % SIDE, tile % 2
    plus = [(i, (i + 1) % groups) for i in range(groups)]
    minus = [(i, (i - 1) % groups) for i in range(groups)]
    both = ("grp", "tile")

    slots = jnp.arange(tile_list.shape[-1], dtype=jnp.int32)
    listed = tile_list[..., None] == jnp.arange(pool, dtype=jnp.int32)
    within = (slots < tile_count[..., None])[..., None]
    live = jnp.any(listed & within, axis=2).astype(jnp.int32)
    table = jnp.concatenate([tile_in[None], live], axis=0)
    other_table = lax.ppermute(table, "tile", swapped())
    rel = jnp.array(REL, jnp.int32)
    along_1, along_2 = jnp.where(core == 0, x, y), jnp.where(core == 0, y, x)
    step_1, step_2 = jnp.where(core == 0, 1, SIDE), jnp.where(core == 0, SIDE, 1)
    place = ((along_2 + rel) % SIDE)[:, None] * step_2 + ((along_1 + rel) % SIDE)[None, :] * step_1
    place = place.reshape(-1).astype(jnp.int32)

    own = amplitudes.reshape(16, amplitudes.shape[-1])
    far = lax.ppermute(own, both, turned(groups, tiles))

    onward = [
        (g * tiles + t, ((g + (-1 if t % 2 else 1)) % groups) * tiles + t)
        for g in range(groups)
        for t in range(tiles)
    ]
    held = jnp.concatenate([integrals, lax.ppermute(integrals, "tile", swapped())], axis=0)
    zero = core == 0
    stays, goes = (jnp.where(zero, held[:, i : i + 8], held[:, 8 - i : 16 - i]) for i in (0, 8))
    own_near = gather(own, 0, (1, -1, 2))
    stays, goes, far, other_table, *own_near = lax.optimization_barrier((stays, goes, far, other_table, *own_near))
    table = jnp.concatenate([table, other_table], axis=1)
    table = jnp.roll(table, (2 - me) * 16, axis=2)
    zero = core == 0
    parts = [table[..., a : a + 8] for a in range(0, 80, 8)]
    order = ((4, 5), (5, 4), (2, 7), (3, 6), (7, 2), (6, 3), (1, 8), (8, 1))
    table = jnp.concatenate([jnp.where(zero, parts[i], parts[j]) for i, j in order], axis=2)
    blocks_in = table[0].reshape(-1)
    live = jnp.transpose(table[1:], (1, 2, 0)).reshape(-1).astype(jnp.float32)
    near_goes = lax.ppermute(goes, both, onward)
    near_stays = lax.ppermute(stays, both, onward)
    half = lax.ppermute(near_goes, both, onward)
    far_amps = spread(far, *gather(far, 0, (1, -1, 2)))
    near_goes, near_stays, own, *own_near = lax.optimization_barrier(
        (near_goes, near_stays, own, *own_near, *far_amps)
    )[:6]
    own_amps = spread(own, *own_near)
    others = [lax.ppermute(x, "tile", swapped()) for x in (near_stays, near_goes)]
    facts = (place, blocks_in, live)
    first, flips, last_flips = [stays, goes, near_stays, near_goes, *others], (0, 0, 0, 0, 1, 1), (0, 1)
    back = partial_ladder(far_amps, first, flips, None, None, False, *facts, pin=True)
    half_other = lax.ppermute(after(half, back, *own_amps[2:6]), "tile", swapped())
    last = [half, half_other]
    back_1 = partial_ladder(far_amps, last, last_flips, 48, back[1:], True, *facts, low=4)
    back_1 = lax.ppermute(back_1[0].astype(jnp.float16), both, turned(groups, tiles))
    back_0 = partial_ladder(far_amps, last, last_flips, 48, back[:1], True, *facts, high=4)
    back_0 = lax.ppermute(back_0[0].astype(jnp.float16), both, turned(groups, tiles))
    every, flips = [*first, *last], (*flips, *last_flips)
    here_0, here_1 = partial_ladder(own_amps, every, flips, None, None, True, *facts)

    other = lax.ppermute((0.5 * (here_1 + back_1.astype(jnp.float32))).astype(jnp.bfloat16), "tile", swapped())
    same = (0.5 * (here_0 + back_0.astype(jnp.float32))).astype(jnp.bfloat16)
    even = jnp.where(zero, same, other).reshape(SIDE * SIDE, 2, 1, 8, 512)
    odd = jnp.where(zero, other, same).reshape(SIDE * SIDE, 2, 1, 8, 512)
    result = jnp.concatenate([even, odd], axis=2).transpose(1, 0, 2, 3, 4)
    return result.reshape(2, 256, 512)


def solution(mesh):
    placed = (
        P(None, ("grp", "tile"), None),
        P("tile", "grp", None, None),
        P("tile", None),
        P(None, "tile", None),
        P(None, "tile"),
    )
    return jax.shard_map(
        functools.partial(on_device, mesh.shape["grp"], mesh.shape["tile"]),
        mesh=mesh,
        in_specs=placed,
        out_specs=P(None, "grp", "tile"),
        check_vma=False,
    )
```

```python
import functools

import jax
import jax.numpy as jnp
from jax import lax
from jax.experimental import pallas as pl
from jax.experimental.pallas import tpu as pltpu
from jax.sharding import PartitionSpec as P

SIDE = 4
REL = (0, -1, 1, 2)
WIDE = 8


def swapped():
    return [(t, t ^ 1) for t in range(SIDE * SIDE * 2)]


def moved(phase, by):
    pairs = []
    for y in range(SIDE):
        for x in range(SIDE):
            for core in range(2):
                along_x = (phase + core) % 2 == 0
                to_y = y if along_x else (y + by) % SIDE
                to_x = (x + by) % SIDE if along_x else x
                pairs.append(((y * SIDE + x) * 2 + core, (to_y * SIDE + to_x) * 2 + core))
    return pairs


def turned(groups, tiles):
    half = groups // 2
    return [
        (g * tiles + t, ((g + half) % groups) * tiles + t)
        for g in range(groups)
        for t in range(tiles)
    ]


def body(pieces, low, tail, ordered, place, blocks_in, live, *refs):
    amps, tiles, out = refs[:pieces], refs[pieces:-1], refs[-1]
    block = low + pl.program_id(0)
    rows = 16 * 16
    first = lax.broadcasted_iota(jnp.int32, (16, 128), 0) < 8
    if tail is None:
        total = jnp.zeros((rows, 128), jnp.float32)
    else:
        tiles, total = tiles[:-1], tiles[-1][0]
    at = tail or 0
    for ref in tiles:
        for chunk in range(ref.shape[1] // WIDE):
            lefts = []
            for j in range(WIDE):
                entry = block * 64 + at + j
                column = pl.multiple_of(blocks_in[entry] * 128, 128)
                mask = jnp.where(first, live[2 * entry], live[2 * entry + 1]).astype(jnp.bfloat16)
                left = [(a[:, :, pl.ds(column, 128)] * mask[None]).reshape(-1, 128) for a in amps]
                lefts.append(jnp.concatenate(left, axis=0))
            left = jnp.concatenate(lefts, axis=1)
            right = ref[0, pl.ds(chunk * WIDE, WIDE)].reshape(WIDE * 128, 128)
            total += jnp.dot(left, right, preferred_element_type=jnp.float32)
            at += WIDE
    if ordered:
        for i in range(16):
            row = pl.multiple_of(place[i] * 16, 16)
            out[0, pl.ds(row, 16), :] = total[16 * i : 16 * (i + 1)]
    else:
        out[0] = total


def partial_ladder(amps, tiles, flips, tail, acc, ordered, place, blocks_in, live, low=0, high=8, light=1, pin=False):
    rows = 256
    count = sum(x.shape[1] for x in tiles)
    if pin:
        amps, tiles = ([pltpu.with_memory_space_constraint(x, pltpu.HBM) for x in xs] for xs in (amps, tiles))

    def tile_map(flip, block, *_):
        return (low + block + 4 * flip) % 8, 0, 0, 0

    def out_map(block, *_):
        return block // 4, 0, block % 4

    specs = [pl.BlockSpec(memory_space=pltpu.VMEM)] * len(amps)
    for x, flip in zip(tiles, flips, strict=True):
        specs.append(pl.BlockSpec((1, *x.shape[1:]), functools.partial(tile_map, flip)))
    if acc is not None:
        specs.append(pl.BlockSpec((1, rows, 128), out_map))
        tiles = [*tiles, acc]
    return pl.pallas_call(
        functools.partial(body, len(amps), low, tail, ordered),
        out_shape=jax.ShapeDtypeStruct(((high - low) // 4, rows, 512), jnp.float32),
        grid_spec=pltpu.PrefetchScalarGridSpec(
            num_scalar_prefetch=3,
            grid=(high - low,),
            in_specs=specs,
            out_specs=pl.BlockSpec((1, rows, 128), out_map),
        ),
        compiler_params=pltpu.CompilerParams(vmem_limit_bytes=24 * 1024 * 1024),
        cost_estimate=pl.CostEstimate(
            flops=2 * rows * count * 128 * 128 * (high - low) // light,
            bytes_accessed=(8 + count * (high - low) // 32) * 1024 * 1024 // light,
            transcendentals=0,
        ),
    )(place, blocks_in, live, *amps, *tiles)


def after(value, *done):
    return lax.optimization_barrier((value, done))[0]


def gather(shard, phase, steps):
    return [lax.ppermute(shard, "tile", moved(phase, step)) for step in steps]


def spread(own, before, behind, opposite):
    fore, aft = jnp.stack([own, before]), jnp.stack([behind, opposite])
    fore_before = lax.ppermute(fore, "tile", moved(1, 1))
    aft_behind = lax.ppermute(aft, "tile", moved(1, -1))
    aft_before = lax.ppermute(aft, "tile", moved(1, 1))
    fore_behind = lax.ppermute(fore, "tile", moved(1, -1))
    fore_beyond = lax.ppermute(fore_before, "tile", moved(1, 1))
    aft_beyond = lax.ppermute(aft_behind, "tile", moved(1, -1))
    return [fore, aft, fore_before, aft_before, fore_behind, aft_behind, fore_beyond, aft_beyond]


def on_device(groups, tiles, amplitudes, integrals, tile_in, tile_list, tile_count):
    pool = tile_in.shape[1]
    me, tile = lax.axis_index("grp"), lax.axis_index("tile")
    y, x, core = tile // (2 * SIDE), (tile // 2) % SIDE, tile % 2
    plus = [(i, (i + 1) % groups) for i in range(groups)]
    minus = [(i, (i - 1) % groups) for i in range(groups)]
    both = ("grp", "tile")

    slots = jnp.arange(tile_list.shape[-1], dtype=jnp.int32)
    listed = tile_list[..., None] == jnp.arange(pool, dtype=jnp.int32)
    within = (slots < tile_count[..., None])[..., None]
    live = jnp.any(listed & within, axis=2).astype(jnp.int32)
    table = jnp.concatenate([tile_in[None], live], axis=0)
    other_table = lax.ppermute(table, "tile", swapped())
    rel = jnp.array(REL, jnp.int32)
    along_1, along_2 = jnp.where(core == 0, x, y), jnp.where(core == 0, y, x)
    step_1, step_2 = jnp.where(core == 0, 1, SIDE), jnp.where(core == 0, SIDE, 1)
    place = ((along_2 + rel) % SIDE)[:, None] * step_2 + ((along_1 + rel) % SIDE)[None, :] * step_1
    place = place.reshape(-1).astype(jnp.int32)

    own = amplitudes.reshape(16, amplitudes.shape[-1])
    far = lax.ppermute(own, both, turned(groups, tiles))

    onward = [
        (g * tiles + t, ((g + (-1 if t % 2 else 1)) % groups) * tiles + t)
        for g in range(groups)
        for t in range(tiles)
    ]
    held = jnp.concatenate([integrals, lax.ppermute(integrals, "tile", swapped())], axis=0)
    zero = core == 0
    stays, goes = (jnp.where(zero, held[:, i : i + 8], held[:, 8 - i : 16 - i]) for i in (0, 8))
    own_near = gather(own, 0, (1, -1, 2))
    stays, goes, far, other_table, *own_near = lax.optimization_barrier((stays, goes, far, other_table, *own_near))
    table = jnp.concatenate([table, other_table], axis=1)
    table = jnp.roll(table, (2 - me) * 16, axis=2)
    zero = core == 0
    parts = [table[..., a : a + 8] for a in range(0, 80, 8)]
    order = ((4, 5), (5, 4), (2, 7), (3, 6), (7, 2), (6, 3), (1, 8), (8, 1))
    table = jnp.concatenate([jnp.where(zero, parts[i], parts[j]) for i, j in order], axis=2)
    blocks_in = table[0].reshape(-1)
    live = jnp.transpose(table[1:], (1, 2, 0)).reshape(-1).astype(jnp.float32)
    near_goes = lax.ppermute(goes, both, onward)
    near_stays = lax.ppermute(stays, both, onward)
    half = lax.ppermute(near_goes, both, onward)
    far_amps = spread(far, *gather(far, 0, (1, -1, 2)))
    near_goes, near_stays, own, *own_near = lax.optimization_barrier(
        (near_goes, near_stays, own, *own_near, *far_amps[:6])
    )[:6]
    own_amps = spread(own, *own_near)
    others = [lax.ppermute(x, "tile", swapped()) for x in (near_stays, near_goes)]
    facts = (place, blocks_in, live)
    first, flips, last_flips = [stays, goes, near_stays, near_goes, *others], (0, 0, 0, 0, 1, 1), (0, 1)
    back = partial_ladder(far_amps, first, flips, None, None, False, *facts, pin=True)
    half_other = lax.ppermute(after(half, back, *own_amps[2:6]), "tile", swapped())
    last = [half, half_other]
    back = partial_ladder(far_amps, last, last_flips, 48, back, True, *facts).astype(jnp.float16)
    back_1 = lax.ppermute(back[1], both, turned(groups, tiles))
    back_0 = lax.ppermute(back[0], both, turned(groups, tiles))
    every, flips = [*first, *last], (*flips, *last_flips)
    here_0, here_1 = partial_ladder(own_amps, every, flips, None, None, True, *facts)

    other = lax.ppermute((0.5 * (here_1 + back_1.astype(jnp.float32))).astype(jnp.bfloat16), "tile", swapped())
    same = (0.5 * (here_0 + back_0.astype(jnp.float32))).astype(jnp.bfloat16)
    even = jnp.where(zero, same, other).reshape(SIDE * SIDE, 2, 1, 8, 512)
    odd = jnp.where(zero, other, same).reshape(SIDE * SIDE, 2, 1, 8, 512)
    result = jnp.concatenate([even, odd], axis=2).transpose(1, 0, 2, 3, 4)
    return result.reshape(2, 256, 512)


def solution(mesh):
    placed = (
        P(None, ("grp", "tile"), None),
        P("tile", "grp", None, None),
        P("tile", None),
        P(None, "tile", None),
        P(None, "tile"),
    )
    return jax.shard_map(
        functools.partial(on_device, mesh.shape["grp"], mesh.shape["tile"]),
        mesh=mesh,
        in_specs=placed,
        out_specs=P(None, "grp", "tile"),
        check_vma=False,
    )
```

```python
import functools

import jax
import jax.numpy as jnp
from jax import lax
from jax.experimental import pallas as pl
from jax.experimental.pallas import tpu as pltpu
from jax.sharding import PartitionSpec as P

SIDE = 4
REL = (0, -1, 1, 2)
WIDE = 8


def swapped():
    return [(t, t ^ 1) for t in range(SIDE * SIDE * 2)]


def moved(phase, by):
    pairs = []
    for y in range(SIDE):
        for x in range(SIDE):
            for core in range(2):
                along_x = (phase + core) % 2 == 0
                to_y = y if along_x else (y + by) % SIDE
                to_x = (x + by) % SIDE if along_x else x
                pairs.append(((y * SIDE + x) * 2 + core, (to_y * SIDE + to_x) * 2 + core))
    return pairs


def turned(groups, tiles):
    half = groups // 2
    return [
        (g * tiles + t, ((g + half) % groups) * tiles + t)
        for g in range(groups)
        for t in range(tiles)
    ]


def body(pieces, low, tail, ordered, place, blocks_in, live, *refs):
    amps, tiles, out = refs[:pieces], refs[pieces:-1], refs[-1]
    block = low + pl.program_id(0)
    rows = 16 * 16
    first = lax.broadcasted_iota(jnp.int32, (16, 128), 0) < 8
    if tail is None:
        total = jnp.zeros((rows, 128), jnp.float32)
    else:
        tiles, total = tiles[:-1], tiles[-1][0]
    at = tail or 0
    for ref in tiles:
        for chunk in range(ref.shape[1] // WIDE):
            lefts = []
            for j in range(WIDE):
                entry = block * 64 + at + j
                column = pl.multiple_of(blocks_in[entry] * 128, 128)
                mask = jnp.where(first, live[2 * entry], live[2 * entry + 1]).astype(jnp.bfloat16)
                left = [(a[:, :, pl.ds(column, 128)] * mask[None]).reshape(-1, 128) for a in amps]
                lefts.append(jnp.concatenate(left, axis=0))
            left = jnp.concatenate(lefts, axis=1)
            right = ref[0, pl.ds(chunk * WIDE, WIDE)].reshape(WIDE * 128, 128)
            total += jnp.dot(left, right, preferred_element_type=jnp.float32)
            at += WIDE
    if ordered:
        for i in range(16):
            row = pl.multiple_of(place[i] * 16, 16)
            out[0, pl.ds(row, 16), :] = total[16 * i : 16 * (i + 1)]
    else:
        out[0] = total


def partial_ladder(amps, tiles, flips, tail, acc, ordered, place, blocks_in, live, low=0, high=8, light=1, pin=False):
    rows = 256
    count = sum(x.shape[1] for x in tiles)
    if pin:
        amps, tiles = ([pltpu.with_memory_space_constraint(x, pltpu.HBM) for x in xs] for xs in (amps, tiles))

    def tile_map(flip, block, *_):
        return (low + block + 4 * flip) % 8, 0, 0, 0

    def out_map(block, *_):
        return block // 4, 0, block % 4

    specs = [pl.BlockSpec(memory_space=pltpu.VMEM)] * len(amps)
    for x, flip in zip(tiles, flips, strict=True):
        specs.append(pl.BlockSpec((1, *x.shape[1:]), functools.partial(tile_map, flip)))
    if acc is not None:
        specs.append(pl.BlockSpec((1, rows, 128), out_map))
        tiles = [*tiles, acc]
    return pl.pallas_call(
        functools.partial(body, len(amps), low, tail, ordered),
        out_shape=jax.ShapeDtypeStruct(((high - low) // 4, rows, 512), jnp.float32),
        grid_spec=pltpu.PrefetchScalarGridSpec(
            num_scalar_prefetch=3,
            grid=(high - low,),
            in_specs=specs,
            out_specs=pl.BlockSpec((1, rows, 128), out_map),
        ),
        compiler_params=pltpu.CompilerParams(vmem_limit_bytes=24 * 1024 * 1024),
        cost_estimate=pl.CostEstimate(
            flops=2 * rows * count * 128 * 128 * (high - low) // light,
            bytes_accessed=(8 + count * (high - low) // 32) * 1024 * 1024 // light,
            transcendentals=0,
        ),
    )(place, blocks_in, live, *amps, *tiles)


def after(value, *done):
    return lax.optimization_barrier((value, done))[0]


def gather(shard, phase, steps):
    return [lax.ppermute(shard, "tile", moved(phase, step)) for step in steps]


def spread(own, before, behind, opposite):
    fore, aft = jnp.stack([own, before]), jnp.stack([behind, opposite])
    fore_before = lax.ppermute(fore, "tile", moved(1, 1))
    aft_behind = lax.ppermute(aft, "tile", moved(1, -1))
    aft_before = lax.ppermute(aft, "tile", moved(1, 1))
    fore_behind = lax.ppermute(fore, "tile", moved(1, -1))
    fore_beyond = lax.ppermute(fore_before, "tile", moved(1, 1))
    aft_beyond = lax.ppermute(aft_behind, "tile", moved(1, -1))
    return [fore, aft, fore_before, aft_before, fore_behind, aft_behind, fore_beyond, aft_beyond]


def on_device(groups, tiles, amplitudes, integrals, tile_in, tile_list, tile_count):
    pool = tile_in.shape[1]
    me, tile = lax.axis_index("grp"), lax.axis_index("tile")
    y, x, core = tile // (2 * SIDE), (tile // 2) % SIDE, tile % 2
    plus = [(i, (i + 1) % groups) for i in range(groups)]
    minus = [(i, (i - 1) % groups) for i in range(groups)]
    both = ("grp", "tile")

    slots = jnp.arange(tile_list.shape[-1], dtype=jnp.int32)
    listed = tile_list[..., None] == jnp.arange(pool, dtype=jnp.int32)
    within = (slots < tile_count[..., None])[..., None]
    live = jnp.any(listed & within, axis=2).astype(jnp.int32)
    table = jnp.concatenate([tile_in[None], live], axis=0)
    other_table = lax.ppermute(table, "tile", swapped())
    rel = jnp.array(REL, jnp.int32)
    along_1, along_2 = jnp.where(core == 0, x, y), jnp.where(core == 0, y, x)
    step_1, step_2 = jnp.where(core == 0, 1, SIDE), jnp.where(core == 0, SIDE, 1)
    place = ((along_2 + rel) % SIDE)[:, None] * step_2 + ((along_1 + rel) % SIDE)[None, :] * step_1
    place = place.reshape(-1).astype(jnp.int32)

    own = amplitudes.reshape(16, amplitudes.shape[-1])
    far = lax.ppermute(own, both, turned(groups, tiles))

    onward = [
        (g * tiles + t, ((g + (-1 if t % 2 else 1)) % groups) * tiles + t)
        for g in range(groups)
        for t in range(tiles)
    ]
    held = jnp.concatenate([integrals, lax.ppermute(integrals, "tile", swapped())], axis=0)
    zero = core == 0
    stays, goes = (jnp.where(zero, held[:, i : i + 8], held[:, 8 - i : 16 - i]) for i in (0, 8))
    own_near = gather(own, 0, (1, -1, 2))
    stays, goes, far, other_table, *own_near = lax.optimization_barrier((stays, goes, far, other_table, *own_near))
    table = jnp.concatenate([table, other_table], axis=1)
    table = jnp.roll(table, (2 - me) * 16, axis=2)
    zero = core == 0
    parts = [table[..., a : a + 8] for a in range(0, 80, 8)]
    order = ((4, 5), (5, 4), (2, 7), (3, 6), (7, 2), (6, 3), (1, 8), (8, 1))
    table = jnp.concatenate([jnp.where(zero, parts[i], parts[j]) for i, j in order], axis=2)
    blocks_in = table[0].reshape(-1)
    live = jnp.transpose(table[1:], (1, 2, 0)).reshape(-1).astype(jnp.float32)
    near_goes = lax.ppermute(goes, both, onward)
    near_stays = lax.ppermute(stays, both, onward)
    half = lax.ppermute(near_goes, both, onward)
    far_amps = spread(far, *gather(far, 0, (1, -1, 2)))
    near_goes, near_stays, own, *own_near = lax.optimization_barrier(
        (near_goes, near_stays, own, *own_near, *far_amps[:2], far_amps[3], far_amps[5])
    )[:6]
    own_amps = spread(own, *own_near)
    others = [lax.ppermute(x, "tile", swapped()) for x in (near_stays, near_goes)]
    facts = (place, blocks_in, live)
    first, flips, last_flips = [stays, goes, near_stays, near_goes, *others], (0, 0, 0, 0, 1, 1), (0, 1)
    back = partial_ladder(far_amps, first, flips, None, None, False, *facts, pin=True)
    half_other = lax.ppermute(after(half, back, *own_amps[2:6]), "tile", swapped())
    last = [half, half_other]
    back = partial_ladder(far_amps, last, last_flips, 48, back, True, *facts).astype(jnp.float16)
    back_1 = lax.ppermute(back[1], both, turned(groups, tiles))
    back_0 = lax.ppermute(back[0], both, turned(groups, tiles))
    every, flips = [*first, *last], (*flips, *last_flips)
    here_0, here_1 = partial_ladder(own_amps, every, flips, None, None, True, *facts)

    other = lax.ppermute((0.5 * (here_1 + back_1.astype(jnp.float32))).astype(jnp.bfloat16), "tile", swapped())
    same = (0.5 * (here_0 + back_0.astype(jnp.float32))).astype(jnp.bfloat16)
    even = jnp.where(zero, same, other).reshape(SIDE * SIDE, 2, 1, 8, 512)
    odd = jnp.where(zero, other, same).reshape(SIDE * SIDE, 2, 1, 8, 512)
    result = jnp.concatenate([even, odd], axis=2).transpose(1, 0, 2, 3, 4)
    return result.reshape(2, 256, 512)


def solution(mesh):
    placed = (
        P(None, ("grp", "tile"), None),
        P("tile", "grp", None, None),
        P("tile", None),
        P(None, "tile", None),
        P(None, "tile"),
    )
    return jax.shard_map(
        functools.partial(on_device, mesh.shape["grp"], mesh.shape["tile"]),
        mesh=mesh,
        in_specs=placed,
        out_specs=P(None, "grp", "tile"),
        check_vma=False,
    )
```
